512 devices in a mesh: gx: 16 (over z), gy: 8 (over y, core), gz: 4 (over x).
Axes of the slice: x: 4, y: 4, z: 16, core: 2. Of those that a mesh axis runs over, the one named last changes fastest.
Arguments:
- positions: float32 [3, 16, 8, 8, 128], P(None, 'gx', 'gy', 'gz'), may hold values from 0 to 16, as said below
- velocity: float32 [3, 16, 8, 8, 128], P(None, 'gx', 'gy', 'gz'), may hold values from -16 to 16
- counts: int32 [16, 8, 8], P('gx', 'gy', 'gz'), may hold values from 0 to 128, as said below
Outputs:
- velocity_new: float32 [3, 16, 8, 8, 128], P(None, 'gx', 'gy', 'gz')
- pressure: float32 [16, 8, 8, 128], P('gx', 'gy', 'gz')
The draws below stay inside these ranges and needn't reach their ends.
Inputs may be any that keep to these rules, and one draw needn't show every extreme that they name: `positions`: component k of the position of any slot of tile (a, b, c) lies in [t, t + 1), where t is a, b or c for k = 0, 1, 2. A tile's particles fill its first counts[a, b, c] slots. In every column of tiles the bottom tile is full, the tiles below one topmost wet tile hold 96 or more particles, and the tiles above it are empty.
All inputs are finite; a program needn't handle non-finite values.
Results may differ from the reference program's by a relative error of at most 0.0003.
Values sent between devices are 32-bit elements; how exact they have to be, the bound alone decides.
A program may use at most 64 MiB of HBM per device.

```python
import math
import jax
import jax.numpy as jnp
from jax import lax

P_SIZE = 128
ITERS = 3
NTX = 16
NTY = 8
NTZ = 8


def draw_positions(key, part):
    unit = jax.random.uniform(key, (3, NTX, NTY, NTZ, P_SIZE), jnp.float32, 0.0, 1.0)
    unit = jnp.minimum(unit, 0.999)
    along_x = jnp.broadcast_to(jnp.arange(NTX, dtype=jnp.float32)[:, None, None], (NTX, NTY, NTZ))
    along_y = jnp.broadcast_to(jnp.arange(NTY, dtype=jnp.float32)[None, :, None], (NTX, NTY, NTZ))
    along_z = jnp.broadcast_to(jnp.arange(NTZ, dtype=jnp.float32)[None, None, :], (NTX, NTY, NTZ))
    corner = jnp.stack([along_x, along_y, along_z])[:, :, :, :, None]
    return (corner + unit).astype(jnp.float32)


def draw_velocity(key, part):
    first_key, second_key = jax.random.split(key, 2)
    ramp = 1.0 + 2.0 * jnp.arange(NTY, dtype=jnp.float32) / NTY
    spread = jax.random.uniform(second_key, (1, NTX, NTY, NTZ, 1), jnp.float32, math.log(0.4), math.log(2.5))
    tile_scale = jnp.exp(spread) * ramp[None, None, :, None, None] / 2.0
    base = jnp.clip(jax.random.normal(first_key, (3, NTX, NTY, NTZ, P_SIZE), jnp.float32), -4.0, 4.0)
    return (base * tile_scale).astype(jnp.float32)


def draw_counts(key, part):
    first_key, second_key = jax.random.split(jax.random.fold_in(key, 17), 2)
    along_x = jnp.arange(NTX, dtype=jnp.int32)[:, None, None]
    along_z = jnp.arange(NTZ, dtype=jnp.int32)[None, None, :]
    surface = NTZ * (9 * NTX - 5 * along_x) // (10 * NTX)
    full_tiles = jnp.minimum(jax.random.randint(first_key, (NTX, NTY, NTZ), P_SIZE - P_SIZE // 4, P_SIZE + P_SIZE // 2), P_SIZE)
    top_tiles = jax.random.randint(second_key, (NTX, NTY, NTZ), 1, P_SIZE + 1)
    filled = jnp.where(along_z < surface, full_tiles, jnp.where(along_z == surface, top_tiles, 0))
    filled = jnp.where(along_z == 0, P_SIZE, filled)
    return filled.astype(jnp.int32)


def setup_inputs(seed: int = 0) -> dict:
    key_list = jax.random.split(jax.random.key(seed), 4)
    positions = draw_positions(jax.random.fold_in(key_list[3], 71), 0)
    velocity = draw_velocity(jax.random.fold_in(key_list[3], 71), 0)
    counts = draw_counts(jax.random.fold_in(key_list[3], 71), 0)
    return {"positions": positions, "velocity": velocity, "counts": counts}


DIAG_SHIFT = 0.05
VISCOSITY = 0.5
GRAVITY = 0.1
GRADIENT_GAIN = 32.0


def tile_pairs(rim_positions, rim_valid, rim_field, fold_step, totals):
    size_x = rim_positions.shape[1] - 2
    size_y = rim_positions.shape[2] - 2
    size_z = rim_positions.shape[3] - 2
    slab_tiles = size_y * size_z
    tile_width = rim_positions.shape[4]

    def near_block(source_array, x_start, y_start, z_start):
        zero_start = jnp.zeros((), jnp.int32)
        window = lax.dynamic_slice(source_array, (zero_start, x_start, y_start, z_start, zero_start), (source_array.shape[0], 1, size_y, size_z, tile_width))
        return window.reshape(source_array.shape[0], slab_tiles, tile_width)

    def slab_totals(x_index):
        unit_step = jnp.ones((), jnp.int32)
        own_positions = near_block(rim_positions, x_index + unit_step, unit_step, unit_step)
        own_valid = near_block(rim_valid, x_index + unit_step, unit_step, unit_step)[0]
        start_totals = jax.tree.map(lambda item: jnp.zeros((item.shape[0], slab_tiles, item.shape[2]), jnp.float32), totals)

        def one_offset(offset_index, carry):
            offset_code = jnp.asarray(offset_index).astype(jnp.int32)
            step_x = offset_code // 9
            step_y = (offset_code // 3) % 3
            step_z = offset_code % 3
            near_positions = near_block(rim_positions, x_index + step_x, step_y, step_z)
            near_valid = near_block(rim_valid, x_index + step_x, step_y, step_z)[0]
            near_field = near_block(rim_field, x_index + step_x, step_y, step_z)
            offset = own_positions[:, :, :, None] - near_positions[:, :, None, :]
            distance = offset[0] * offset[0] + offset[1] * offset[1] + offset[2] * offset[2]
            closeness = jnp.maximum(1.0 - distance, 0.0)
            weight = closeness * closeness * own_valid[:, :, None] * near_valid[:, None, :]
            return fold_step(carry, weight, offset, near_field)

        return lax.fori_loop(0, 27, one_offset, start_totals)

    stacked = lax.map(slab_totals, jnp.arange(size_x, dtype=jnp.int32))
    return jax.tree.map(lambda block_out: jnp.moveaxis(block_out, 0, 1).reshape(block_out.shape[1], size_x * slab_tiles, block_out.shape[3]), stacked)


def flat_zeros(rim_positions, components):
    tile_count = (rim_positions.shape[1] - 2) * (rim_positions.shape[2] - 2) * (rim_positions.shape[3] - 2)
    return jnp.zeros((components, tile_count, rim_positions.shape[4]), jnp.float32)


def unflat(flat_values, rim_positions):
    return flat_values.reshape(flat_values.shape[0], rim_positions.shape[1] - 2, rim_positions.shape[2] - 2, rim_positions.shape[3] - 2, flat_values.shape[2])


def viscous_fold(totals, weight, offset, near_field):
    near_sums, row_sums = totals
    near_sums = near_sums + jnp.einsum("tij,ctj->cti", weight, near_field, precision=lax.Precision.HIGHEST)
    return (near_sums, row_sums + jnp.sum(weight, axis=2)[None])


def divergence_fold(totals, weight, offset, near_field):
    lever_sums, flux_sums = totals
    levered = weight[None] * offset
    flux_sums = flux_sums + jnp.einsum("ctij,ctj->ti", levered, near_field, precision=lax.Precision.HIGHEST)[None]
    return (lever_sums + jnp.sum(levered, axis=3), flux_sums)


def laplace_fold(totals, weight, offset, near_field):
    return totals + jnp.einsum("tij,ctj->cti", weight, near_field, precision=lax.Precision.HIGHEST)


def gradient_fold(totals, weight, offset, near_field):
    levered = weight[None] * offset
    return totals + jnp.einsum("ctij,tj->cti", levered, near_field[0], precision=lax.Precision.HIGHEST)


def viscous_pass(rim_positions, rim_valid, rim_field):
    near_sums, row_sums = tile_pairs(rim_positions, rim_valid, rim_field, viscous_fold, (flat_zeros(rim_positions, 3), flat_zeros(rim_positions, 1)))
    return unflat(near_sums, rim_positions), unflat(row_sums, rim_positions)


def divergence_pass(rim_positions, rim_valid, rim_field):
    lever_sums, flux_sums = tile_pairs(rim_positions, rim_valid, rim_field, divergence_fold, (flat_zeros(rim_positions, 3), flat_zeros(rim_positions, 1)))
    return unflat(lever_sums, rim_positions), unflat(flux_sums, rim_positions)


def laplace_pass(rim_positions, rim_valid, rim_field):
    return unflat(tile_pairs(rim_positions, rim_valid, rim_field, laplace_fold, flat_zeros(rim_positions, 1)), rim_positions)


def gradient_pass(rim_positions, rim_valid, rim_field):
    return unflat(tile_pairs(rim_positions, rim_valid, rim_field, gradient_fold, flat_zeros(rim_positions, 3)), rim_positions)


def advance(velocity, valid_mask, near_sums, row_sums):
    gravity_pull = jnp.array([0.0, 0.0, -GRAVITY], jnp.float32).reshape(3, 1, 1, 1, 1)
    return valid_mask * (velocity + VISCOSITY / P_SIZE * (near_sums - row_sums * velocity) + gravity_pull)


def padded_grid(field):
    return jnp.pad(field, ((0, 0), (1, 1), (1, 1), (1, 1), (0, 0)))


def sweep_slabs(function, padded):
    def slab_view(slab_index):
        return function(*[lax.dynamic_slice_in_dim(item, slab_index, 3, 1) for item in padded])

    stacked = lax.map(slab_view, jnp.arange(NTX, dtype=jnp.int32))
    return jax.tree.map(lambda block_out: jnp.moveaxis(block_out, 0, 1).reshape((block_out.shape[1], NTX) + block_out.shape[3:]), stacked)


def reference(positions, velocity, counts):
    slot_ids = jnp.arange(P_SIZE, dtype=jnp.int32)
    valid_mask = (slot_ids[None, None, None, :] < counts[:, :, :, None]).astype(jnp.float32)[None]
    pad_positions = padded_grid(positions)
    pad_valid = padded_grid(valid_mask)
    near_sums, row_sums = sweep_slabs(viscous_pass, [pad_positions, pad_valid, padded_grid(velocity)])
    predicted = advance(velocity, valid_mask, near_sums, row_sums)
    diagonal = DIAG_SHIFT + row_sums / P_SIZE
    lever_sums, flux_sums = sweep_slabs(divergence_pass, [pad_positions, pad_valid, padded_grid(predicted)])
    source = -(GRADIENT_GAIN / P_SIZE) * (jnp.sum(predicted * lever_sums, axis=0, keepdims=True) - flux_sums)
    pressure = jnp.zeros_like(source)
    residual = source
    precond = residual / diagonal
    direction = precond
    norm_now = jnp.sum(residual * precond)
    for iteration in range(ITERS):
        applied = diagonal * direction - sweep_slabs(laplace_pass, [pad_positions, pad_valid, padded_grid(direction)]) / P_SIZE
        step_size = norm_now / jnp.sum(direction * applied)
        pressure = pressure + step_size * direction
        residual = residual - step_size * applied
        if iteration + 1 < ITERS:
            precond = residual / diagonal
            norm_next = jnp.sum(residual * precond)
            direction = precond + (norm_next / norm_now) * direction
            norm_now = norm_next
    moments = sweep_slabs(gradient_pass, [pad_positions, pad_valid, padded_grid(pressure)])
    velocity_new = predicted - (GRADIENT_GAIN / P_SIZE) * (pressure * lever_sums - moments)
    return velocity_new, pressure[0]
```

```python
import functools
import itertools

import jax
import jax.numpy as jnp
from jax import lax
from jax.experimental import pallas as pl
from jax.experimental.pallas import tpu as pltpu
from jax.sharding import PartitionSpec as P

P_SIZE = 128
DIAG_SHIFT = 0.05
VISCOSITY = 0.5
GRAVITY = 0.1
GRADIENT_GAIN = 32.0

MESH = pl.DeviceIdType.MESH
F32 = jnp.float32
AXES = ("gx", "gy", "gz")
OFFSETS = sorted((o for o in itertools.product((-1, 0, 1), repeat=3) if any(o)), key=lambda o: -sum(map(abs, o)))
N_OFF = len(OFFSETS)
OWN = 17
GROUPS = (
    ((0, 0),),
    ((-1, 0), (1, 0), (0, -1), (0, 1)),
    ((-1, -1), (-1, 1), (1, -1), (1, 1)),
)


def near_index(column, step_z):
    return ((column[0] + 1) * 3 + column[1] + 1) * 3 + step_z


def tile_index(column, own, step_z):
    return ((column[0] + 1) * 3 + column[1] + 1) * 4 + own + step_z


ALL_COLUMNS = tuple(c for g in GROUPS for c in g)


def kernel(sizes, pos, vel, counts, vel_out, pres_out, x_own, x_halo, x_col, weights, sums, cols, p_own, p_halo, t_own,
           t_halo, levered, a_own, a_halo, b_own, b_halo, send, recv, a_sem, b_sem):
    me = [lax.axis_index(axis) for axis in AXES]

    def device(offset):
        return tuple(lax.rem(m + (d + n), n) for m, d, n in zip(me, offset, sizes))

    plane = [(0, a, b) for a in range(sizes[1]) for b in range(sizes[2]) if a or b]
    length = [(a, 0, 0) for a in range(1, sizes[0])]
    inside = {
        (1, -1): me[1] > 0, (1, 1): me[1] < sizes[1] - 1,
        (2, -1): me[2] > 0, (2, 1): me[2] < sizes[2] - 1,
    }

    def exists(dy, dz):
        terms = [inside[axis, d] for axis, d in ((1, dy), (2, dz)) if d]
        if not terms:
            return None
        return terms[0] if len(terms) == 1 else jnp.logical_and(*terms)

    def under(condition, body):
        if condition is None:
            body()
        else:
            pl.when(condition)(body)

    x_halo[...] = jnp.zeros_like(x_halo)
    p_halo[...] = jnp.zeros_like(p_halo)
    t_halo[...] = jnp.zeros_like(t_halo)

    barrier = pltpu.get_barrier_semaphore()
    greeted = OFFSETS + [(3, 0, 0), (-3, 0, 0)]
    for offset in greeted:
        pl.semaphore_signal(barrier, inc=1, device_id=device(offset), device_id_type=MESH)

    lanes = lax.broadcasted_iota(jnp.int32, (1, P_SIZE), 1)
    valid = [(lanes < counts[t]).astype(F32) for t in range(2)]
    for t in range(2):
        for k in range(3):
            x_own[t, k : k + 1] = pos[k, t : t + 1]
            x_own[t, 3 + k : 4 + k] = vel[k, t : t + 1]
        x_own[t, 6:7] = valid[t]
        x_own[t, 7:8] = jnp.zeros((1, P_SIZE), F32)
        x_halo[OWN + t] = x_own[t]
        for k in range(3):
            x_col[t, k] = jnp.broadcast_to(pos[k, t : t + 1], (P_SIZE, P_SIZE)).T
    pl.semaphore_wait(barrier, len(greeted))

    def copy(phase, own, halo, offset):
        dx, dy, dz = offset
        place = ((1 - dx) * 3 + 1 - dy) * 4
        if dz == 0:
            source, target = own, halo.at[place + 1 : place + 3]
        elif dz > 0:
            source, target = own.at[1:2], halo.at[place : place + 1]
        else:
            source, target = own.at[0:1], halo.at[place + 3 : place + 4]
        i = OFFSETS.index(offset)
        return pltpu.make_async_remote_copy(
            source, target, send.at[phase, i], recv.at[phase, i], device_id=device(offset), device_id_type=MESH
        )

    combos = sorted(itertools.product((-1, 0, 1), repeat=2), key=lambda c: -sum(map(abs, c)))

    def start(phase, own, halo):
        for dy, dz in combos:
            def body(dy=dy, dz=dz):
                for dx in (-1, 1, 0):
                    if dx or dy or dz:
                        copy(phase, own, halo, (dx, dy, dz)).start()
            under(exists(dy, dz), body)

    def arrive(phase, own, halo, columns):
        for dy, dz in combos[::-1]:
            steps = [-c[0] for c in columns if c[1] == -dy and (c[0] or dy or dz)]
            if steps:
                def body(dy=dy, dz=dz, steps=steps):
                    for dx in steps:
                        copy(phase, own, halo, (dx, dy, dz)).wait_recv()
                under(exists(-dy, -dz), body)

    def sent(phase, own, halo):
        for dy, dz in combos:
            def body(dy=dy, dz=dz):
                for dx in (-1, 1, 0):
                    if dx or dy or dz:
                        copy(phase, own, halo, (dx, dy, dz)).wait_send()
            under(exists(dy, dz), body)

    def to_rows(n):
        for r in range(0, P_SIZE, 16):
            block = jnp.zeros((16, P_SIZE), F32)
            for a in range(2):
                for q in range(n):
                    total = jnp.sum(sums[a, q, r : r + 16], axis=1, keepdims=True)
                    block = jnp.where(lanes == 16 * a + q, total, block)
            cols[r : r + 16] = block
        turned = cols[...].T
        return [[turned[16 * a + q : 16 * a + q + 1] for q in range(n)] for a in range(2)]

    def apply(n, row_of, depth):
        @pl.loop(0, P_SIZE // depth)
        def _(block):
            at = pl.ds(pl.multiple_of(block * depth, depth), depth)
            for a in range(2):
                totals = [jnp.zeros((depth, P_SIZE), F32)] * n
                for column in ALL_COLUMNS:
                    for dz in range(3):
                        tile = tile_index(column, a, dz)
                        w = weights[a, near_index(column, dz), at]
                        for q in range(n):
                            totals[q] = totals[q] + w * row_of(tile, q)
                for q in range(n):
                    sums[a, q, at] = totals[q]
        return to_rows(n)

    start(0, x_own, x_halo)
    for number, columns in enumerate(GROUPS):
        arrive(0, x_own, x_halo, columns)

        @pl.loop(0, P_SIZE // 16)
        def _(block, number=number, columns=columns):
            at = pl.ds(pl.multiple_of(block * 16, 16), 16)
            for a in range(2):
                mine = [x_col[a, k, at] for k in range(3)]
                if number:
                    totals = [sums[a, q, at] for q in range(7)]
                else:
                    totals = [jnp.zeros((16, P_SIZE), F32)] * 7
                for column in columns:
                    for dz in range(3):
                        tile = tile_index(column, a, dz)
                        d = [mine[k] - x_halo[tile, k : k + 1] for k in range(3)]
                        near = jnp.maximum(1.0 - (d[0] * d[0] + d[1] * d[1] + d[2] * d[2]), 0.0)
                        w = near * near * x_halo[tile, 6:7]
                        weights[a, near_index(column, dz), at] = w
                        totals[0] = totals[0] + w
                        for k in range(3):
                            totals[1 + k] = totals[1 + k] + w * x_halo[tile, 3 + k : 4 + k]
                            totals[4 + k] = totals[4 + k] + w * d[k]
                for q in range(7):
                    sums[a, q, at] = totals[q]

    rows = to_rows(7)
    scale = 1.0 / P_SIZE
    centre = [s * 0.5 for s in (sizes[0], sizes[1], sizes[2] * 2)]
    diagonal, lever, predicted, x = [], [], [], []
    for a in range(2):
        row = rows[a][0] * valid[a]
        v = [vel[k, a : a + 1] for k in range(3)]
        x.append([pos[k, a : a + 1] - centre[k] for k in range(3)])
        diagonal.append(DIAG_SHIFT + row * scale)
        lever.append([rows[a][4 + k] * valid[a] for k in range(3)])
        p = [valid[a] * (v[k] + VISCOSITY * scale * (rows[a][1 + k] - row * v[k]) - (GRAVITY if k == 2 else 0.0)) for k in range(3)]
        predicted.append(p)
        for k in range(3):
            p_own[a, k : k + 1] = p[k]
        p_own[a, 3:4] = p[0] * x[a][0] + p[1] * x[a][1] + p[2] * x[a][2]
    start(1, p_own, p_halo)
    p_halo[OWN : OWN + 2] = p_own[...]
    arrive(1, p_own, p_halo, ALL_COLUMNS)
    rows = apply(4, lambda tile, q: p_halo[tile, q : q + 1], 16)
    basis, source = [[], [], [], []], []
    for a in range(2):
        flux = x[a][0] * rows[a][0] + x[a][1] * rows[a][1] + x[a][2] * rows[a][2] - rows[a][3]
        dot = predicted[a][0] * lever[a][0] + predicted[a][1] * lever[a][1] + predicted[a][2] * lever[a][2]
        source.append(valid[a] * (-(GRADIENT_GAIN * scale) * (dot - flux)))
        basis[0].append(source[a] / diagonal[a])
        t_own[0, a] = basis[0][a]
    inverse = [scale * valid[a] / diagonal[a] for a in range(2)]

    spread = []
    for k in range(3):
        start(2 + k, t_own.at[k], t_halo.at[k])
        t_halo[k, OWN : OWN + 2] = t_own[k]
        arrive(2 + k, t_own.at[k], t_halo.at[k], ALL_COLUMNS)
        rows = apply(1, lambda tile, q, k=k: t_halo[k, tile], 32)
        spread.append([rows[a][0] for a in range(2)])
        for a in range(2):
            basis[k + 1].append(spread[k][a] * inverse[a])
            if k < 2:
                t_own[k + 1, a] = basis[k + 1][a]

    packed = jnp.zeros((1, P_SIZE), F32)
    for q in range(6):
        i, j = q // 2, (q + 1) // 2
        terms = sum(diagonal[a] * basis[i][a] * basis[j][a] for a in range(2))
        packed = jnp.where(lanes == q, jnp.sum(terms, axis=1, keepdims=True), packed)

    def share(peers, own, halo, sem):
        for i, offset in enumerate(peers):
            pltpu.make_async_remote_copy(
                own, halo.at[i : i + 1], sem.at[0], sem.at[1], device_id=device(offset), device_id_type=MESH
            ).start()

    def gathered(peers, own, halo, sem):
        pltpu.make_async_copy(halo, halo, sem.at[1]).wait()
        return own[0] + jnp.sum(halo[...], axis=0)

    a_own[0] = packed
    share(plane, a_own, a_halo, a_sem)

    for tile in range(36):
        local = x_halo[tile]
        for c in range(3):
            levered[c, tile] = (local[c : c + 1] - centre[c]) * jnp.concatenate([t_halo[k, tile] for k in range(3)] + [jnp.zeros((5, P_SIZE), F32)], axis=0)
    rows = apply(9, lambda tile, q: levered[q // 3, tile, q % 3 : q % 3 + 1], 16)
    moved = []
    for a in range(2):
        moved.append([
            [basis[k][a] * lever[a][c] - valid[a] * (x[a][c] * spread[k][a] - rows[a][3 * c + k]) for k in range(3)]
            for c in range(3)
        ])

    b_own[0] = gathered(plane, a_own, a_halo, a_sem)
    share(length, b_own, b_halo, b_sem)
    sent(0, x_own, x_halo)
    sent(1, p_own, p_halo)
    for k in range(3):
        sent(2 + k, t_own.at[k], t_halo.at[k])
    pltpu.make_async_copy(a_halo, a_halo, a_sem.at[0]).wait()
    total = gathered(length, b_own, b_halo, b_sem)

    m = [jnp.sum(jnp.where(lanes == q, total, 0.0), axis=1, keepdims=True) for q in range(6)]
    g00, g01, g11, g12, g22 = (m[q] - m[q + 1] for q in range(5))
    l1, l2 = g01 / g00, g11 / g00
    a11, a12, a22 = g11 - l1 * g01, g12 - l1 * g11, g22 - l2 * g11
    y1, y2 = m[1] - l1 * m[0], m[2] - l2 * m[0]
    l3 = a12 / a11
    c2 = (y2 - l3 * y1) / (a22 - l3 * a12)
    c1 = (y1 - a12 * c2) / a11
    c0 = (m[0] - g01 * c1 - g11 * c2) / g00
    weight = [c0, c1, c2]
    for a in range(2):
        pres_out[a : a + 1] = sum(weight[k] * basis[k][a] for k in range(3))
        for c in range(3):
            vel_out[c, a : a + 1] = predicted[a][c] - (GRADIENT_GAIN * scale) * sum(weight[k] * moved[a][c][k] for k in range(3))
    pltpu.make_async_copy(b_halo, b_halo, b_sem.at[0]).wait()


def solution(mesh):
    sizes = tuple(mesh.shape[axis] for axis in AXES)

    def on_device(positions, velocity, counts):
        vmem = pl.BlockSpec(memory_space=pltpu.VMEM)
        n_plane, n_length = sizes[1] * sizes[2] - 1, sizes[0] - 1
        moved, pressure = pl.pallas_call(
            functools.partial(kernel, sizes),
            out_shape=(jax.ShapeDtypeStruct((3, 2, P_SIZE), F32), jax.ShapeDtypeStruct((2, P_SIZE), F32)),
            in_specs=[vmem, vmem, pl.BlockSpec(memory_space=pltpu.SMEM)],
            out_specs=(vmem, vmem),
            scratch_shapes=[
                pltpu.VMEM((2, 8, P_SIZE), F32),
                pltpu.VMEM((36, 8, P_SIZE), F32),
                pltpu.VMEM((2, 3, P_SIZE, P_SIZE), F32),
                pltpu.VMEM((2, 27, P_SIZE, P_SIZE), F32),
                pltpu.VMEM((2, 9, P_SIZE, P_SIZE), F32),
                pltpu.VMEM((P_SIZE, P_SIZE), F32),
                pltpu.VMEM((2, 4, P_SIZE), F32),
                pltpu.VMEM((36, 4, P_SIZE), F32),
                pltpu.VMEM((3, 2, 1, P_SIZE), F32),
                pltpu.VMEM((3, 36, 1, P_SIZE), F32),
                pltpu.VMEM((3, 36, 8, P_SIZE), F32),
                pltpu.VMEM((1, 1, P_SIZE), F32),
                pltpu.VMEM((n_plane, 1, P_SIZE), F32),
                pltpu.VMEM((1, 1, P_SIZE), F32),
                pltpu.VMEM((n_length, 1, P_SIZE), F32),
                pltpu.SemaphoreType.DMA((5, N_OFF)),
                pltpu.SemaphoreType.DMA((5, N_OFF)),
                pltpu.SemaphoreType.DMA((2,)),
                pltpu.SemaphoreType.DMA((2,)),
            ],
            compiler_params=pltpu.CompilerParams(
                collective_id=0, has_side_effects=True, vmem_limit_bytes=32 * 1024 * 1024
            ),
            name="project",
        )(positions.reshape(3, 2, P_SIZE), velocity.reshape(3, 2, P_SIZE), counts.reshape(2))
        return moved.reshape(3, 1, 1, 2, P_SIZE), pressure.reshape(1, 1, 2, P_SIZE)

    return jax.shard_map(
        on_device,
        mesh=mesh,
        in_specs=(P(None, *AXES, None), P(None, *AXES, None), P(*AXES)),
        out_specs=(P(None, *AXES, None), P(*AXES, None)),
        check_vma=False,
    )
```

```python
import functools
import itertools

import jax
import jax.numpy as jnp
from jax import lax
from jax.experimental import pallas as pl
from jax.experimental.pallas import tpu as pltpu
from jax.sharding import PartitionSpec as P

P_SIZE = 128
AWAY = 64.0
DIAG_SHIFT = 0.05
VISCOSITY = 0.5
GRAVITY = 0.1
GRADIENT_GAIN = 32.0

MESH = pl.DeviceIdType.MESH
F32 = jnp.float32
AXES = ("gx", "gy", "gz")
OFFSETS = sorted((o for o in itertools.product((-1, 0, 1), repeat=3) if any(o)), key=lambda o: -sum(map(abs, o)))
N_OFF = len(OFFSETS)
OWN = 17


def pairs(own, hops):
    found = []
    for column in range(9):
        for step in range(3):
            across = abs(column // 3 - 1) + abs(column % 3 - 1) + (own + step in (0, 3))
            if across in hops:
                found.append((column * 4 + own + step, column * 3 + step))
    return found


ALL = (0, 1, 2, 3)


def kernel(sizes, pos_in, vel_in, counts_in, vel_out, pres_out, pos, vel, counts, load, x_own, x_halo, x_col, weights, sums, cols, p_own, p_halo, t_own, t_sums,
           t_halo, levered, a_own, a_halo, b_own, b_halo, send, recv, a_sem, b_sem):
    me = [lax.axis_index(axis) for axis in AXES]

    def device(offset):
        return tuple(lax.rem(m + (d + n), n) if d else m for m, d, n in zip(me, offset, sizes))

    loads = [
        pltpu.make_async_copy(a, b, load.at[i]) for i, (a, b) in enumerate(((pos_in, pos), (vel_in, vel), (counts_in, counts)))
    ]
    for item in loads:
        item.start()

    plane = [(0, a, b) for a in range(sizes[1]) for b in range(sizes[2]) if a or b]
    length = [(a, 0, 0) for a in range(1, sizes[0])]
    inside = {
        (1, -1): me[1] > 0, (1, 1): me[1] < sizes[1] - 1,
        (2, -1): me[2] > 0, (2, 1): me[2] < sizes[2] - 1,
    }

    def exists(dy, dz):
        terms = [inside[axis, d] for axis, d in ((1, dy), (2, dz)) if d]
        if not terms:
            return None
        return terms[0] if len(terms) == 1 else jnp.logical_and(*terms)

    def under(condition, body):
        if condition is None:
            body()
        else:
            pl.when(condition)(body)

    x_halo[...] = jnp.full_like(x_halo, AWAY)

    barrier = pltpu.get_barrier_semaphore()
    greeted = OFFSETS + [(3, 0, 0), (-3, 0, 0)]
    for offset in greeted:
        pl.semaphore_signal(barrier, inc=1, device_id=device(offset), device_id_type=MESH)

    p_halo[...] = jnp.zeros_like(p_halo)
    t_halo[...] = jnp.zeros_like(t_halo)
    for item in loads:
        item.wait()
    lanes = lax.broadcasted_iota(jnp.int32, (1, P_SIZE), 1)
    valid = [(lanes < counts[t]).astype(F32) for t in range(2)]
    for t in range(2):
        for k in range(3):
            x_own[t, k : k + 1] = jnp.where(valid[t] > 0, pos[k, t : t + 1], AWAY)
            x_own[t, 3 + k : 4 + k] = vel[k, t : t + 1]
        x_own[t, 6:8] = jnp.zeros((2, P_SIZE), F32)
        x_halo[OWN + t] = x_own[t]
        for k in range(3):
            x_col[t, k] = jnp.broadcast_to(pos[k, t : t + 1], (P_SIZE, P_SIZE)).T
    pl.semaphore_wait(barrier, len(greeted))

    def copy(phase, own, halo, offset):
        dx, dy, dz = offset
        place = ((1 - dx) * 3 + 1 - dy) * 4
        if dz == 0:
            source, target = own, halo.at[place + 1 : place + 3]
        elif dz > 0:
            source, target = own.at[1:2], halo.at[place : place + 1]
        else:
            source, target = own.at[0:1], halo.at[place + 3 : place + 4]
        i = OFFSETS.index(offset)
        return pltpu.make_async_remote_copy(
            source, target, send.at[phase, i], recv.at[phase, i], device_id=device(offset), device_id_type=MESH
        )

    combos = sorted(itertools.product((-1, 0, 1), repeat=2), key=lambda c: -sum(map(abs, c)))

    def start(phase, own, halo):
        for dy, dz in combos:
            def body(dy=dy, dz=dz):
                for dx in (-1, 1, 0):
                    if dx or dy or dz:
                        copy(phase, own, halo, (dx, dy, dz)).start()
            under(exists(dy, dz), body)

    def arrive(phase, own, halo, hops):
        for dy, dz in combos[::-1]:
            steps = [dx for dx in (-1, 0, 1) if abs(dx) + abs(dy) + abs(dz) == hops]
            if steps and hops:
                def body(dy=dy, dz=dz, steps=steps):
                    for dx in steps:
                        copy(phase, own, halo, (dx, dy, dz)).wait_recv()
                under(exists(-dy, -dz), body)

    def sent(phase, own, halo):
        for dy, dz in combos:
            def body(dy=dy, dz=dz):
                for dx in (-1, 1, 0):
                    if dx or dy or dz:
                        copy(phase, own, halo, (dx, dy, dz)).wait_send()
            under(exists(dy, dz), body)

    def to_rows(n):
        for r in range(0, P_SIZE, 16):
            block = jnp.zeros((16, P_SIZE), F32)
            for a in range(2):
                for q in range(n):
                    total = jnp.sum(sums[a, q, r : r + 16], axis=1, keepdims=True)
                    block = jnp.where(lanes == 16 * a + q, total, block)
            cols[r : r + 16] = block
        turned = cols[...].T
        return [[turned[16 * a + q : 16 * a + q + 1] for q in range(n)] for a in range(2)]

    def apply(n, term, depth, exchange=None):
        for hops in ((0,), (1,), (2,), (3,)) if exchange else (ALL,):
            if exchange:
                arrive(*exchange, hops[0])

            @pl.loop(0, P_SIZE // depth)
            def _(block, hops=hops):
                at = pl.ds(pl.multiple_of(block * depth, depth), depth)
                for a in range(2):
                    if hops[0]:
                        totals = [sums[a, q, at] for q in range(n)]
                    else:
                        totals = [jnp.zeros((depth, P_SIZE), F32)] * n
                    for tile, place in pairs(a, hops):
                        terms = term(a, at, tile, place)
                        for q in range(n):
                            totals[q] = totals[q] + terms[q]
                    for q in range(n):
                        sums[a, q, at] = totals[q]
        return to_rows(n)

    def offset(a, at, tile):
        return [x_col[a, k, at] - x_halo[tile, k : k + 1] for k in range(3)]

    def weigh(a, at, tile, place):
        d = offset(a, at, tile)
        near = jnp.maximum(1.0 - (d[0] * d[0] + d[1] * d[1] + d[2] * d[2]), 0.0)
        w = near * near
        weights[a, place, at] = w
        return [w] + [w * x_halo[tile, 3 + k : 4 + k] for k in range(3)]

    def lever_terms(a, at, tile, place):
        w = weights[a, place, at]
        return [w * d for d in offset(a, at, tile)]

    def times(n, row_of):
        def term(a, at, tile, place):
            w = weights[a, place, at]
            return [w * row_of(tile, q) for q in range(n)]
        return term

    start(0, x_own, x_halo)
    rows = apply(4, weigh, 16, (0, x_own, x_halo))
    scale = 1.0 / P_SIZE
    centre = [s * 0.5 for s in (sizes[0], sizes[1], sizes[2] * 2)]
    diagonal, predicted, x = [], [], []
    for a in range(2):
        row = rows[a][0] * valid[a]
        v = [vel[k, a : a + 1] for k in range(3)]
        x.append([pos[k, a : a + 1] - centre[k] for k in range(3)])
        diagonal.append(DIAG_SHIFT + row * scale)
        p = [valid[a] * (v[k] + VISCOSITY * scale * (rows[a][1 + k] - row * v[k]) - (GRAVITY if k == 2 else 0.0)) for k in range(3)]
        predicted.append(p)
        for k in range(3):
            p_own[a, k : k + 1] = p[k]
        p_own[a, 3:4] = p[0] * x[a][0] + p[1] * x[a][1] + p[2] * x[a][2]
    start(1, p_own, p_halo)
    p_halo[OWN : OWN + 2] = p_own[...]
    rows = apply(3, lever_terms, 16)
    lever = [[rows[a][k] * valid[a] for k in range(3)] for a in range(2)]
    rows = apply(4, times(4, lambda tile, q: p_halo[tile, q : q + 1]), 64, (1, p_own, p_halo))
    for a in range(2):
        flux = x[a][0] * rows[a][0] + x[a][1] * rows[a][1] + x[a][2] * rows[a][2] - rows[a][3]
        dot = predicted[a][0] * lever[a][0] + predicted[a][1] * lever[a][1] + predicted[a][2] * lever[a][2]
        t_own[0, a] = valid[a] * (-(GRADIENT_GAIN * scale) * (dot - flux)) / diagonal[a]
    inverse = [scale * valid[a] / diagonal[a] for a in range(2)]

    @pl.loop(0, 3)
    def _(k):
        own, halo = t_own.at[k], t_halo.at[k]
        start(2 + k, own, halo)
        halo[OWN : OWN + 2] = own[...]
        rows = apply(1, times(1, lambda tile, q: halo[tile]), 64, (2 + k, own, halo))
        for a in range(2):
            t_sums[k, a] = rows[a][0]
            t_own[k + 1, a] = rows[a][0] * inverse[a]

    basis = [[t_own[k, a] for a in range(2)] for k in range(4)]
    spread = [[t_sums[k, a] for a in range(2)] for k in range(3)]
    packed = jnp.zeros((1, P_SIZE), F32)
    for q in range(6):
        i, j = q // 2, (q + 1) // 2
        terms = sum(diagonal[a] * basis[i][a] * basis[j][a] for a in range(2))
        packed = jnp.where(lanes == q, jnp.sum(terms, axis=1, keepdims=True), packed)

    def share(peers, own, halo, sem):
        for i, offset in enumerate(peers):
            pltpu.make_async_remote_copy(
                own, halo.at[i : i + 1], sem.at[0], sem.at[1], device_id=device(offset), device_id_type=MESH
            ).start()

    def gathered(peers, own, halo, sem):
        pltpu.make_async_copy(halo, halo, sem.at[1]).wait()
        return own[0] + jnp.sum(halo[...], axis=0)

    a_own[0] = packed
    share(plane, a_own, a_halo, a_sem)

    for tile in range(36):
        local = x_halo[tile]
        for c in range(3):
            levered[c, tile] = (local[c : c + 1] - centre[c]) * jnp.concatenate([t_halo[k, tile] for k in range(3)] + [jnp.zeros((5, P_SIZE), F32)], axis=0)
    rows = apply(9, times(9, lambda tile, q: levered[q // 3, tile, q % 3 : q % 3 + 1]), 16)
    moved = []
    for a in range(2):
        moved.append([
            [basis[k][a] * lever[a][c] - valid[a] * (x[a][c] * spread[k][a] - rows[a][3 * c + k]) for k in range(3)]
            for c in range(3)
        ])

    b_own[0] = gathered(plane, a_own, a_halo, a_sem)
    share(length, b_own, b_halo, b_sem)
    sent(0, x_own, x_halo)
    sent(1, p_own, p_halo)

    @pl.loop(0, 3)
    def _(k):
        sent(2 + k, t_own.at[k], t_halo.at[k])

    pltpu.make_async_copy(a_halo, a_halo, a_sem.at[0]).wait()
    total = gathered(length, b_own, b_halo, b_sem)

    m = [jnp.sum(jnp.where(lanes == q, total, 0.0), axis=1, keepdims=True) for q in range(6)]
    g00, g01, g11, g12, g22 = (m[q] - m[q + 1] for q in range(5))
    l1, l2 = g01 / g00, g11 / g00
    a11, a12, a22 = g11 - l1 * g01, g12 - l1 * g11, g22 - l2 * g11
    y1, y2 = m[1] - l1 * m[0], m[2] - l2 * m[0]
    l3 = a12 / a11
    c2 = (y2 - l3 * y1) / (a22 - l3 * a12)
    c1 = (y1 - a12 * c2) / a11
    c0 = (m[0] - g01 * c1 - g11 * c2) / g00
    weight = [c0, c1, c2]
    for a in range(2):
        pres_out[a : a + 1] = sum(weight[k] * basis[k][a] for k in range(3))
        for c in range(3):
            vel_out[c, a : a + 1] = predicted[a][c] - (GRADIENT_GAIN * scale) * sum(weight[k] * moved[a][c][k] for k in range(3))
    pltpu.make_async_copy(b_halo, b_halo, b_sem.at[0]).wait()


def solution(mesh):
    sizes = tuple(mesh.shape[axis] for axis in AXES)

    def on_device(positions, velocity, counts):
        vmem = pl.BlockSpec(memory_space=pltpu.VMEM)
        n_plane, n_length = sizes[1] * sizes[2] - 1, sizes[0] - 1
        moved, pressure = pl.pallas_call(
            functools.partial(kernel, sizes),
            out_shape=(jax.ShapeDtypeStruct((3, 2, P_SIZE), F32), jax.ShapeDtypeStruct((2, P_SIZE), F32)),
            in_specs=[pl.BlockSpec(memory_space=pltpu.HBM)] * 3,
            out_specs=(vmem, vmem),
            scratch_shapes=[
                pltpu.VMEM((3, 2, P_SIZE), F32),
                pltpu.VMEM((3, 2, P_SIZE), F32),
                pltpu.SMEM((2,), jnp.int32),
                pltpu.SemaphoreType.DMA((3,)),
                pltpu.VMEM((2, 8, P_SIZE), F32),
                pltpu.VMEM((36, 8, P_SIZE), F32),
                pltpu.VMEM((2, 3, P_SIZE, P_SIZE), F32),
                pltpu.VMEM((2, 27, P_SIZE, P_SIZE), F32),
                pltpu.VMEM((2, 9, P_SIZE, P_SIZE), F32),
                pltpu.VMEM((P_SIZE, P_SIZE), F32),
                pltpu.VMEM((2, 4, P_SIZE), F32),
                pltpu.VMEM((36, 4, P_SIZE), F32),
                pltpu.VMEM((4, 2, 1, P_SIZE), F32),
                pltpu.VMEM((3, 2, 1, P_SIZE), F32),
                pltpu.VMEM((3, 36, 1, P_SIZE), F32),
                pltpu.VMEM((3, 36, 8, P_SIZE), F32),
                pltpu.VMEM((1, 1, P_SIZE), F32),
                pltpu.VMEM((n_plane, 1, P_SIZE), F32),
                pltpu.VMEM((1, 1, P_SIZE), F32),
                pltpu.VMEM((n_length, 1, P_SIZE), F32),
                pltpu.SemaphoreType.DMA((5, N_OFF)),
                pltpu.SemaphoreType.DMA((5, N_OFF)),
                pltpu.SemaphoreType.DMA((2,)),
                pltpu.SemaphoreType.DMA((2,)),
            ],
            compiler_params=pltpu.CompilerParams(
                collective_id=0, has_side_effects=True, vmem_limit_bytes=55220 * 1024
            ),
            name="project",
        )(positions.reshape(3, 2, P_SIZE), velocity.reshape(3, 2, P_SIZE), counts.reshape(2))
        return moved.reshape(3, 1, 1, 2, P_SIZE), pressure.reshape(1, 1, 2, P_SIZE)

    return jax.shard_map(
        on_device,
        mesh=mesh,
        in_specs=(P(None, *AXES, None), P(None, *AXES, None), P(*AXES)),
        out_specs=(P(None, *AXES, None), P(*AXES, None)),
        check_vma=False,
    )
```

```python
import functools
import itertools

import jax
import jax.numpy as jnp
from jax import lax
from jax.experimental import pallas as pl
from jax.experimental.pallas import tpu as pltpu
from jax.sharding import PartitionSpec as P

P_SIZE = 128
AWAY = 64.0
DIAG_SHIFT = 0.05
VISCOSITY = 0.5
GRAVITY = 0.1
GRADIENT_GAIN = 32.0

MESH = pl.DeviceIdType.MESH
F32 = jnp.float32
AXES = ("gx", "gy", "gz")
OFFSETS = sorted((o for o in itertools.product((-1, 0, 1), repeat=3) if any(o)), key=lambda o: -sum(map(abs, o)))
N_OFF = len(OFFSETS)
OWN = 17


def pairs(own, hops):
    found = []
    for column in range(9):
        for step in range(3):
            across = abs(column // 3 - 1) + abs(column % 3 - 1) + (own + step in (0, 3))
            if across in hops:
                found.append((column * 4 + own + step, column * 3 + step))
    return found


ALL = (0, 1, 2, 3)


def kernel(sizes, pos_in, vel_in, counts_in, vel_out, pres_out, pos, vel, counts, load, x_own, x_halo, x_col, weights, sums, cols, p_own, p_halo, t_own, t_sums,
           t_halo, levered, a_own, a_halo, b_own, b_halo, send, recv, a_sem, b_sem):
    me = [lax.axis_index(axis) for axis in AXES]

    def device(offset):
        return tuple(lax.rem(m + (d + n), n) if d else m for m, d, n in zip(me, offset, sizes))

    loads = [
        pltpu.make_async_copy(a, b, load.at[i]) for i, (a, b) in enumerate(((pos_in, pos), (vel_in, vel), (counts_in, counts)))
    ]
    for item in loads:
        item.start()

    def far(offset):
        return -sum(min(d, n - d) for d, n in zip(offset, sizes))

    plane = sorted(((0, a, b) for a in range(sizes[1]) for b in range(sizes[2]) if a or b), key=far)
    length = sorted(((a, 0, 0) for a in range(1, sizes[0])), key=far)
    inside = {
        (1, -1): me[1] > 0, (1, 1): me[1] < sizes[1] - 1,
        (2, -1): me[2] > 0, (2, 1): me[2] < sizes[2] - 1,
    }

    def exists(dy, dz):
        terms = [inside[axis, d] for axis, d in ((1, dy), (2, dz)) if d]
        if not terms:
            return None
        return terms[0] if len(terms) == 1 else jnp.logical_and(*terms)

    def under(condition, body):
        if condition is None:
            body()
        else:
            pl.when(condition)(body)

    x_halo[...] = jnp.full_like(x_halo, AWAY)

    barrier = pltpu.get_barrier_semaphore()
    greeted = OFFSETS + [(3, 0, 0), (-3, 0, 0)]
    for offset in greeted:
        pl.semaphore_signal(barrier, inc=1, device_id=device(offset), device_id_type=MESH)

    p_halo[...] = jnp.zeros_like(p_halo)
    t_halo[...] = jnp.zeros_like(t_halo)
    for item in loads:
        item.wait()
    lanes = lax.broadcasted_iota(jnp.int32, (1, P_SIZE), 1)
    valid = [(lanes < counts[t]).astype(F32) for t in range(2)]
    for t in range(2):
        for k in range(3):
            x_own[t, k : k + 1] = jnp.where(valid[t] > 0, pos[k, t : t + 1], AWAY)
            x_own[t, 3 + k : 4 + k] = vel[k, t : t + 1]
        x_own[t, 6:8] = jnp.zeros((2, P_SIZE), F32)
    pl.semaphore_wait(barrier, len(greeted))

    def copy(phase, own, halo, offset):
        dx, dy, dz = offset
        place = ((1 - dx) * 3 + 1 - dy) * 4
        if dz == 0:
            source, target = own, halo.at[place + 1 : place + 3]
        elif dz > 0:
            source, target = own.at[1:2], halo.at[place : place + 1]
        else:
            source, target = own.at[0:1], halo.at[place + 3 : place + 4]
        i = OFFSETS.index(offset)
        return pltpu.make_async_remote_copy(
            source, target, send.at[phase, i], recv.at[phase, i], device_id=device(offset), device_id_type=MESH
        )

    combos = sorted(itertools.product((-1, 0, 1), repeat=2), key=lambda c: sum(map(abs, c)))

    def start(phase, own, halo):
        for dy, dz in combos:
            def body(dy=dy, dz=dz):
                for dx in (0, -1, 1):
                    if dx or dy or dz:
                        copy(phase, own, halo, (dx, dy, dz)).start()
            under(exists(dy, dz), body)

    def arrive(phase, own, halo, hops):
        for dy, dz in combos:
            steps = [dx for dx in (-1, 0, 1) if abs(dx) + abs(dy) + abs(dz) == hops]
            if steps and hops:
                def body(dy=dy, dz=dz, steps=steps):
                    for dx in steps:
                        copy(phase, own, halo, (dx, dy, dz)).wait_recv()
                under(exists(-dy, -dz), body)

    def sent(phase, own, halo):
        for dy, dz in combos:
            def body(dy=dy, dz=dz):
                for dx in (-1, 1, 0):
                    if dx or dy or dz:
                        copy(phase, own, halo, (dx, dy, dz)).wait_send()
            under(exists(dy, dz), body)

    def to_rows(n):
        for r in range(0, P_SIZE, 16):
            block = jnp.zeros((16, P_SIZE), F32)
            for a in range(2):
                for q in range(n):
                    total = jnp.sum(sums[a, q, r : r + 16], axis=1, keepdims=True)
                    block = jnp.where(lanes == 16 * a + q, total, block)
            cols[r : r + 16] = block
        turned = cols[...].T
        return [[turned[16 * a + q : 16 * a + q + 1] for q in range(n)] for a in range(2)]

    def apply(n, term, depth, exchange=None):
        for hops in ((0,), (1,), (2,), (3,)) if exchange else (ALL,):
            if exchange:
                arrive(*exchange, hops[0])

            @pl.loop(0, P_SIZE // depth)
            def _(block, hops=hops):
                at = pl.ds(pl.multiple_of(block * depth, depth), depth)
                for a in range(2):
                    if hops[0]:
                        totals = [sums[a, q, at] for q in range(n)]
                    else:
                        totals = [jnp.zeros((depth, P_SIZE), F32)] * n
                    for tile, place in pairs(a, hops):
                        terms = term(a, at, tile, place)
                        for q in range(n):
                            totals[q] = totals[q] + terms[q]
                    for q in range(n):
                        sums[a, q, at] = totals[q]
        return to_rows(n)

    def offset(a, at, tile):
        return [x_col[a, k, at] - x_halo[tile, k : k + 1] for k in range(3)]

    def weigh(a, at, tile, place):
        d = offset(a, at, tile)
        near = jnp.maximum(1.0 - (d[0] * d[0] + d[1] * d[1] + d[2] * d[2]), 0.0)
        w = near * near
        weights[a, place, at] = w
        return [w] + [w * x_halo[tile, 3 + k : 4 + k] for k in range(3)]

    def lever_terms(a, at, tile, place):
        w = weights[a, place, at]
        return [w * d for d in offset(a, at, tile)]

    def times(n, row_of):
        def term(a, at, tile, place):
            w = weights[a, place, at]
            return [w * row_of(tile, q) for q in range(n)]
        return term

    start(0, x_own, x_halo)
    for t in range(2):
        x_halo[OWN + t] = x_own[t]
        for k in range(3):
            x_col[t, k] = jnp.broadcast_to(pos[k, t : t + 1], (P_SIZE, P_SIZE)).T
    rows = apply(4, weigh, 16, (0, x_own, x_halo))
    scale = 1.0 / P_SIZE
    centre = [s * 0.5 for s in (sizes[0], sizes[1], sizes[2] * 2)]
    diagonal, predicted, x = [], [], []
    for a in range(2):
        row = rows[a][0] * valid[a]
        v = [vel[k, a : a + 1] for k in range(3)]
        x.append([pos[k, a : a + 1] - centre[k] for k in range(3)])
        diagonal.append(DIAG_SHIFT + row * scale)
        p = [valid[a] * (v[k] + VISCOSITY * scale * (rows[a][1 + k] - row * v[k]) - (GRAVITY if k == 2 else 0.0)) for k in range(3)]
        predicted.append(p)
        for k in range(3):
            p_own[a, k : k + 1] = p[k]
        p_own[a, 3:4] = p[0] * x[a][0] + p[1] * x[a][1] + p[2] * x[a][2]
    start(1, p_own, p_halo)
    p_halo[OWN : OWN + 2] = p_own[...]
    rows = apply(3, lever_terms, 16)
    lever = [[rows[a][k] * valid[a] for k in range(3)] for a in range(2)]
    rows = apply(4, times(4, lambda tile, q: p_halo[tile, q : q + 1]), 64, (1, p_own, p_halo))
    for a in range(2):
        flux = x[a][0] * rows[a][0] + x[a][1] * rows[a][1] + x[a][2] * rows[a][2] - rows[a][3]
        dot = predicted[a][0] * lever[a][0] + predicted[a][1] * lever[a][1] + predicted[a][2] * lever[a][2]
        t_own[0, a] = valid[a] * (-(GRADIENT_GAIN * scale) * (dot - flux)) / diagonal[a]
    inverse = [scale * valid[a] / diagonal[a] for a in range(2)]

    @pl.loop(0, 3)
    def _(k):
        own, halo = t_own.at[k], t_halo.at[k]
        start(2 + k, own, halo)
        halo[OWN : OWN + 2] = own[...]
        rows = apply(1, times(1, lambda tile, q: halo[tile]), 64, (2 + k, own, halo))
        for a in range(2):
            t_sums[k, a] = rows[a][0]
            t_own[k + 1, a] = rows[a][0] * inverse[a]

    basis = [[t_own[k, a] for a in range(2)] for k in range(4)]
    spread = [[t_sums[k, a] for a in range(2)] for k in range(3)]
    packed = jnp.zeros((1, P_SIZE), F32)
    for q in range(6):
        i, j = q // 2, (q + 1) // 2
        terms = sum(diagonal[a] * basis[i][a] * basis[j][a] for a in range(2))
        packed = jnp.where(lanes == q, jnp.sum(terms, axis=1, keepdims=True), packed)

    def share(peers, own, halo, sem):
        for i, offset in enumerate(peers):
            pltpu.make_async_remote_copy(
                own, halo.at[i : i + 1], sem.at[0], sem.at[1], device_id=device(offset), device_id_type=MESH
            ).start()

    def gathered(peers, own, halo, sem):
        pltpu.make_async_copy(halo, halo, sem.at[1]).wait()
        return own[0] + jnp.sum(halo[...], axis=0)

    a_own[0] = packed
    share(plane, a_own, a_halo, a_sem)

    for tile in range(36):
        local = x_halo[tile]
        for c in range(3):
            levered[c, tile] = (local[c : c + 1] - centre[c]) * jnp.concatenate([t_halo[k, tile] for k in range(3)] + [jnp.zeros((5, P_SIZE), F32)], axis=0)
    rows = apply(9, times(9, lambda tile, q: levered[q // 3, tile, q % 3 : q % 3 + 1]), 16)
    moved = []
    for a in range(2):
        moved.append([
            [basis[k][a] * lever[a][c] - valid[a] * (x[a][c] * spread[k][a] - rows[a][3 * c + k]) for k in range(3)]
            for c in range(3)
        ])

    b_own[0] = gathered(plane, a_own, a_halo, a_sem)
    share(length, b_own, b_halo, b_sem)
    sent(0, x_own, x_halo)
    sent(1, p_own, p_halo)

    @pl.loop(0, 3)
    def _(k):
        sent(2 + k, t_own.at[k], t_halo.at[k])

    pltpu.make_async_copy(a_halo, a_halo, a_sem.at[0]).wait()
    total = gathered(length, b_own, b_halo, b_sem)

    m = [jnp.sum(jnp.where(lanes == q, total, 0.0), axis=1, keepdims=True) for q in range(6)]
    g00, g01, g11, g12, g22 = (m[q] - m[q + 1] for q in range(5))
    l1, l2 = g01 / g00, g11 / g00
    a11, a12, a22 = g11 - l1 * g01, g12 - l1 * g11, g22 - l2 * g11
    y1, y2 = m[1] - l1 * m[0], m[2] - l2 * m[0]
    l3 = a12 / a11
    c2 = (y2 - l3 * y1) / (a22 - l3 * a12)
    c1 = (y1 - a12 * c2) / a11
    c0 = (m[0] - g01 * c1 - g11 * c2) / g00
    weight = [c0, c1, c2]
    for a in range(2):
        pres_out[a : a + 1] = sum(weight[k] * basis[k][a] for k in range(3))
        for c in range(3):
            vel_out[c, a : a + 1] = predicted[a][c] - (GRADIENT_GAIN * scale) * sum(weight[k] * moved[a][c][k] for k in range(3))
    pltpu.make_async_copy(b_halo, b_halo, b_sem.at[0]).wait()


def solution(mesh):
    sizes = tuple(mesh.shape[axis] for axis in AXES)

    def on_device(positions, velocity, counts):
        vmem = pl.BlockSpec(memory_space=pltpu.VMEM)
        n_plane, n_length = sizes[1] * sizes[2] - 1, sizes[0] - 1
        moved, pressure = pl.pallas_call(
            functools.partial(kernel, sizes),
            out_shape=(jax.ShapeDtypeStruct((3, 2, P_SIZE), F32), jax.ShapeDtypeStruct((2, P_SIZE), F32)),
            in_specs=[pl.BlockSpec(memory_space=pltpu.HBM)] * 3,
            out_specs=(vmem, vmem),
            scratch_shapes=[
                pltpu.VMEM((3, 2, P_SIZE), F32),
                pltpu.VMEM((3, 2, P_SIZE), F32),
                pltpu.SMEM((2,), jnp.int32),
                pltpu.SemaphoreType.DMA((3,)),
                pltpu.VMEM((2, 8, P_SIZE), F32),
                pltpu.VMEM((36, 8, P_SIZE), F32),
                pltpu.VMEM((2, 3, P_SIZE, P_SIZE), F32),
                pltpu.VMEM((2, 27, P_SIZE, P_SIZE), F32),
                pltpu.VMEM((2, 9, P_SIZE, P_SIZE), F32),
                pltpu.VMEM((P_SIZE, P_SIZE), F32),
                pltpu.VMEM((2, 4, P_SIZE), F32),
                pltpu.VMEM((36, 4, P_SIZE), F32),
                pltpu.VMEM((4, 2, 1, P_SIZE), F32),
                pltpu.VMEM((3, 2, 1, P_SIZE), F32),
                pltpu.VMEM((3, 36, 1, P_SIZE), F32),
                pltpu.VMEM((3, 36, 8, P_SIZE), F32),
                pltpu.VMEM((1, 1, P_SIZE), F32),
                pltpu.VMEM((n_plane, 1, P_SIZE), F32),
                pltpu.VMEM((1, 1, P_SIZE), F32),
                pltpu.VMEM((n_length, 1, P_SIZE), F32),
                pltpu.SemaphoreType.DMA((5, N_OFF)),
                pltpu.SemaphoreType.DMA((5, N_OFF)),
                pltpu.SemaphoreType.DMA((2,)),
                pltpu.SemaphoreType.DMA((2,)),
            ],
            compiler_params=pltpu.CompilerParams(
                collective_id=0, has_side_effects=True, vmem_limit_bytes=32 * 1024 * 1024
            ),
            name="project",
        )(*(pltpu.with_memory_space_constraint(v, pltpu.HBM) for v in (positions.reshape(3, 2, P_SIZE), velocity.reshape(3, 2, P_SIZE), counts.reshape(2))))
        return moved.reshape(3, 1, 1, 2, P_SIZE), pressure.reshape(1, 1, 2, P_SIZE)

    return jax.shard_map(
        on_device,
        mesh=mesh,
        in_specs=(P(None, *AXES, None), P(None, *AXES, None), P(*AXES)),
        out_specs=(P(None, *AXES, None), P(*AXES, None)),
        check_vma=False,
    )
```

```python
import functools
import itertools

import jax
import jax.numpy as jnp
from jax import lax
from jax.experimental import pallas as pl
from jax.experimental.pallas import tpu as pltpu
from jax.sharding import PartitionSpec as P

P_SIZE = 128
AWAY = 64.0
DIAG_SHIFT = 0.05
VISCOSITY = 0.5
GRAVITY = 0.1
GRADIENT_GAIN = 32.0

MESH = pl.DeviceIdType.MESH
F32 = jnp.float32
AXES = ("gx", "gy", "gz")
OFFSETS = sorted((o for o in itertools.product((-1, 0, 1), repeat=3) if any(o)), key=lambda o: -sum(map(abs, o)))
N_OFF = len(OFFSETS)
OWN = 17


def pairs(own, hops):
    found = []
    for column in range(9):
        for step in range(3):
            across = abs(column // 3 - 1) + abs(column % 3 - 1) + (own + step in (0, 3))
            if across in hops:
                found.append((column * 4 + own + step, column * 3 + step))
    return found


ALL = (0, 1, 2, 3)


def kernel(sizes, pos_in, vel_in, counts_in, vel_out, pres_out, pos, vel, counts, load, x_own, x_halo, x_col, weights, sums, cols, p_own, p_halo, t_own, t_sums,
           t_halo, levered, a_own, a_halo, b_own, b_halo, send, recv, a_sem, b_sem):
    me = [lax.axis_index(axis) for axis in AXES]

    def device(offset):
        return tuple(lax.rem(m + (d + n), n) if d else m for m, d, n in zip(me, offset, sizes))

    loads = [
        pltpu.make_async_copy(a, b, load.at[i]) for i, (a, b) in enumerate(((pos_in, pos), (vel_in, vel), (counts_in, counts)))
    ]
    for item in loads:
        item.start()

    def far(offset):
        return -sum(min(d, n - d) for d, n in zip(offset, sizes))

    plane = sorted(((0, a, b) for a in range(sizes[1]) for b in range(sizes[2]) if a or b), key=far)
    length = sorted(((a, 0, 0) for a in range(1, sizes[0])), key=far)
    inside = {
        (1, -1): me[1] > 0, (1, 1): me[1] < sizes[1] - 1,
        (2, -1): me[2] > 0, (2, 1): me[2] < sizes[2] - 1,
    }

    def exists(dy, dz):
        terms = [inside[axis, d] for axis, d in ((1, dy), (2, dz)) if d]
        if not terms:
            return None
        return terms[0] if len(terms) == 1 else jnp.logical_and(*terms)

    def under(condition, body):
        if condition is None:
            body()
        else:
            pl.when(condition)(body)

    x_halo[...] = jnp.full_like(x_halo, AWAY)

    barrier = pltpu.get_barrier_semaphore()
    greeted = OFFSETS + [(3, 0, 0), (-3, 0, 0)]
    for offset in greeted:
        pl.semaphore_signal(barrier, inc=1, device_id=device(offset), device_id_type=MESH)

    p_halo[...] = jnp.zeros_like(p_halo)
    t_halo[...] = jnp.zeros_like(t_halo)
    for item in loads:
        item.wait()
    lanes = lax.broadcasted_iota(jnp.int32, (1, P_SIZE), 1)
    valid = [(lanes < counts[t]).astype(F32) for t in range(2)]
    for t in range(2):
        for k in range(3):
            x_own[t, k : k + 1] = jnp.where(valid[t] > 0, pos[k, t : t + 1], AWAY)
            x_own[t, 3 + k : 4 + k] = vel[k, t : t + 1]
        x_own[t, 6:8] = jnp.zeros((2, P_SIZE), F32)
    pl.semaphore_wait(barrier, len(greeted))

    def copy(phase, own, halo, offset):
        dx, dy, dz = offset
        place = ((1 - dx) * 3 + 1 - dy) * 4
        if dz == 0:
            source, target = own, halo.at[place + 1 : place + 3]
        elif dz > 0:
            source, target = own.at[1:2], halo.at[place : place + 1]
        else:
            source, target = own.at[0:1], halo.at[place + 3 : place + 4]
        i = OFFSETS.index(offset)
        return pltpu.make_async_remote_copy(
            source, target, send.at[phase, i], recv.at[phase, i], device_id=device(offset), device_id_type=MESH
        )

    combos = sorted(itertools.product((-1, 0, 1), repeat=2), key=lambda c: sum(map(abs, c)))

    def start(phase, own, halo):
        for dy, dz in combos:
            def body(dy=dy, dz=dz):
                for dx in (0, -1, 1):
                    if dx or dy or dz:
                        copy(phase, own, halo, (dx, dy, dz)).start()
            under(exists(dy, dz), body)

    def arrive(phase, own, halo, hops):
        for dy, dz in combos:
            steps = [dx for dx in (-1, 0, 1) if abs(dx) + abs(dy) + abs(dz) == hops]
            if steps and hops:
                def body(dy=dy, dz=dz, steps=steps):
                    for dx in steps:
                        copy(phase, own, halo, (dx, dy, dz)).wait_recv()
                under(exists(-dy, -dz), body)

    def sent(phase, own, halo):
        for dy, dz in combos:
            def body(dy=dy, dz=dz):
                for dx in (-1, 1, 0):
                    if dx or dy or dz:
                        copy(phase, own, halo, (dx, dy, dz)).wait_send()
            under(exists(dy, dz), body)

    def to_rows(n):
        for r in range(0, P_SIZE, 16):
            block = jnp.zeros((16, P_SIZE), F32)
            for a in range(2):
                for q in range(n):
                    total = jnp.sum(sums[a, q, r : r + 16], axis=1, keepdims=True)
                    block = jnp.where(lanes == 16 * a + q, total, block)
            cols[r : r + 16] = block
        turned = cols[...].T
        return [[turned[16 * a + q : 16 * a + q + 1] for q in range(n)] for a in range(2)]

    def apply(n, term, depth, exchange=None):
        for hops in ((0,), (1,), (2,), (3,)) if exchange else (ALL,):
            if exchange:
                arrive(*exchange, hops[0])

            @pl.loop(0, P_SIZE // depth)
            def _(block, hops=hops):
                at = pl.ds(pl.multiple_of(block * depth, depth), depth)
                for a in range(2):
                    if hops[0]:
                        totals = [sums[a, q, at] for q in range(n)]
                    else:
                        totals = [jnp.zeros((depth, P_SIZE), F32)] * n
                    for tile, place in pairs(a, hops):
                        terms = term(a, at, tile, place)
                        for q in range(n):
                            totals[q] = totals[q] + terms[q]
                    for q in range(n):
                        sums[a, q, at] = totals[q]
        return to_rows(n)

    def offset(a, at, tile):
        return [x_col[a, k, at] - x_halo[tile, k : k + 1] for k in range(3)]

    def weigh(a, at, tile, place):
        d = offset(a, at, tile)
        near = jnp.maximum(1.0 - (d[0] * d[0] + d[1] * d[1] + d[2] * d[2]), 0.0)
        w = near * near
        weights[a, place, at] = w
        return [w] + [w * x_halo[tile, 3 + k : 4 + k] for k in range(3)]

    def lever_terms(a, at, tile, place):
        w = weights[a, place, at]
        return [w * d for d in offset(a, at, tile)]

    def times(n, row_of):
        def term(a, at, tile, place):
            w = weights[a, place, at]
            return [w * row_of(tile, q) for q in range(n)]
        return term

    start(0, x_own, x_halo)
    for t in range(2):
        x_halo[OWN + t] = x_own[t]
        for k in range(3):
            x_col[t, k] = jnp.broadcast_to(pos[k, t : t + 1], (P_SIZE, P_SIZE)).T
    rows = apply(4, weigh, 16, (0, x_own, x_halo))
    scale = 1.0 / P_SIZE
    centre = [s * 0.5 for s in (sizes[0], sizes[1], sizes[2] * 2)]
    diagonal, predicted, x = [], [], []
    for a in range(2):
        row = rows[a][0] * valid[a]
        v = [vel[k, a : a + 1] for k in range(3)]
        x.append([pos[k, a : a + 1] - centre[k] for k in range(3)])
        diagonal.append(DIAG_SHIFT + row * scale)
        p = [valid[a] * (v[k] + VISCOSITY * scale * (rows[a][1 + k] - row * v[k]) - (GRAVITY if k == 2 else 0.0)) for k in range(3)]
        predicted.append(p)
        for k in range(3):
            p_own[a, k : k + 1] = p[k]
        p_own[a, 3:4] = p[0] * x[a][0] + p[1] * x[a][1] + p[2] * x[a][2]
    start(1, p_own, p_halo)
    p_halo[OWN : OWN + 2] = p_own[...]
    rows = apply(3, lever_terms, 16)
    lever = [[rows[a][k] * valid[a] for k in range(3)] for a in range(2)]
    rows = apply(4, times(4, lambda tile, q: p_halo[tile, q : q + 1]), 64, (1, p_own, p_halo))
    for a in range(2):
        flux = x[a][0] * rows[a][0] + x[a][1] * rows[a][1] + x[a][2] * rows[a][2] - rows[a][3]
        dot = predicted[a][0] * lever[a][0] + predicted[a][1] * lever[a][1] + predicted[a][2] * lever[a][2]
        t_own[0, a] = valid[a] * (-(GRADIENT_GAIN * scale) * (dot - flux)) / diagonal[a]
    inverse = [scale * valid[a] / diagonal[a] for a in range(2)]

    @pl.loop(0, 3)
    def _(k):
        own, halo = t_own.at[k], t_halo.at[k]
        start(2 + k, own, halo)
        halo[OWN : OWN + 2] = own[...]
        rows = apply(1, times(1, lambda tile, q: halo[tile]), 64, (2 + k, own, halo))
        for a in range(2):
            t_sums[k, a] = rows[a][0]
            t_own[k + 1, a] = rows[a][0] * inverse[a]

    basis = [[t_own[k, a] for a in range(2)] for k in range(4)]
    spread = [[t_sums[k, a] for a in range(2)] for k in range(3)]
    packed = jnp.zeros((1, P_SIZE), F32)
    for q in range(6):
        i, j = q // 2, (q + 1) // 2
        terms = sum(diagonal[a] * basis[i][a] * basis[j][a] for a in range(2))
        packed = jnp.where(lanes == q, jnp.sum(terms, axis=1, keepdims=True), packed)

    def share(peers, own, halo, sem):
        for i, offset in enumerate(peers):
            pltpu.make_async_remote_copy(
                own, halo.at[i : i + 1], sem.at[0], sem.at[1], device_id=device(offset), device_id_type=MESH
            ).start()

    def gathered(peers, own, halo, sem):
        pltpu.make_async_copy(halo, halo, sem.at[1]).wait()
        return own[0] + jnp.sum(halo[...], axis=0)

    a_own[0] = packed
    share(plane, a_own, a_halo, a_sem)

    for tile in range(36):
        local = x_halo[tile]
        for c in range(3):
            levered[c, tile] = (local[c : c + 1] - centre[c]) * jnp.concatenate([t_halo[k, tile] for k in range(3)] + [jnp.zeros((5, P_SIZE), F32)], axis=0)
    rows = apply(9, times(9, lambda tile, q: levered[q // 3, tile, q % 3 : q % 3 + 1]), 16)
    moved = []
    for a in range(2):
        moved.append([
            [basis[k][a] * lever[a][c] - valid[a] * (x[a][c] * spread[k][a] - rows[a][3 * c + k]) for k in range(3)]
            for c in range(3)
        ])

    b_own[0] = gathered(plane, a_own, a_halo, a_sem)
    share(length, b_own, b_halo, b_sem)
    sent(0, x_own, x_halo)
    sent(1, p_own, p_halo)

    @pl.loop(0, 3)
    def _(k):
        sent(2 + k, t_own.at[k], t_halo.at[k])

    pltpu.make_async_copy(a_halo, a_halo, a_sem.at[0]).wait()
    total = gathered(length, b_own, b_halo, b_sem)

    m = [jnp.sum(jnp.where(lanes == q, total, 0.0), axis=1, keepdims=True) for q in range(6)]
    g00, g01, g11, g12, g22 = (m[q] - m[q + 1] for q in range(5))
    l1, l2 = g01 / g00, g11 / g00
    a11, a12, a22 = g11 - l1 * g01, g12 - l1 * g11, g22 - l2 * g11
    y1, y2 = m[1] - l1 * m[0], m[2] - l2 * m[0]
    l3 = a12 / a11
    c2 = (y2 - l3 * y1) / (a22 - l3 * a12)
    c1 = (y1 - a12 * c2) / a11
    c0 = (m[0] - g01 * c1 - g11 * c2) / g00
    weight = [c0, c1, c2]
    for a in range(2):
        pres_out[a : a + 1] = sum(weight[k] * basis[k][a] for k in range(3))
        for c in range(3):
            vel_out[c, a : a + 1] = predicted[a][c] - (GRADIENT_GAIN * scale) * sum(weight[k] * moved[a][c][k] for k in range(3))
    pltpu.make_async_copy(b_halo, b_halo, b_sem.at[0]).wait()


def solution(mesh):
    sizes = tuple(mesh.shape[axis] for axis in AXES)

    def on_device(positions, velocity, counts):
        vmem = pl.BlockSpec(memory_space=pltpu.VMEM)
        n_plane, n_length = sizes[1] * sizes[2] - 1, sizes[0] - 1
        moved, pressure = pl.pallas_call(
            functools.partial(kernel, sizes),
            out_shape=(jax.ShapeDtypeStruct((3, 2, P_SIZE), F32), jax.ShapeDtypeStruct((2, P_SIZE), F32)),
            in_specs=[pl.BlockSpec(memory_space=pltpu.HBM)] * 3,
            out_specs=(vmem, vmem),
            scratch_shapes=[
                pltpu.VMEM((3, 2, P_SIZE), F32),
                pltpu.VMEM((3, 2, P_SIZE), F32),
                pltpu.SMEM((2,), jnp.int32),
                pltpu.SemaphoreType.DMA((3,)),
                pltpu.VMEM((2, 8, P_SIZE), F32),
                pltpu.VMEM((36, 8, P_SIZE), F32),
                pltpu.VMEM((2, 3, P_SIZE, P_SIZE), F32),
                pltpu.VMEM((2, 27, P_SIZE, P_SIZE), F32),
                pltpu.VMEM((2, 9, P_SIZE, P_SIZE), F32),
                pltpu.VMEM((P_SIZE, P_SIZE), F32),
                pltpu.VMEM((2, 4, P_SIZE), F32),
                pltpu.VMEM((36, 4, P_SIZE), F32),
                pltpu.VMEM((4, 2, 1, P_SIZE), F32),
                pltpu.VMEM((3, 2, 1, P_SIZE), F32),
                pltpu.VMEM((3, 36, 1, P_SIZE), F32),
                pltpu.VMEM((3, 36, 8, P_SIZE), F32),
                pltpu.VMEM((1, 1, P_SIZE), F32),
                pltpu.VMEM((n_plane, 1, P_SIZE), F32),
                pltpu.VMEM((1, 1, P_SIZE), F32),
                pltpu.VMEM((n_length, 1, P_SIZE), F32),
                pltpu.SemaphoreType.DMA((5, N_OFF)),
                pltpu.SemaphoreType.DMA((5, N_OFF)),
                pltpu.SemaphoreType.DMA((2,)),
                pltpu.SemaphoreType.DMA((2,)),
            ],
            compiler_params=pltpu.CompilerParams(
                collective_id=0, has_side_effects=True, vmem_limit_bytes=32 * 1024 * 1024
            ),
            name="project",
        )(*(pltpu.with_memory_space_constraint(v, pltpu.HBM) for v in (positions.reshape(3, 2, P_SIZE), velocity.reshape(3, 2, P_SIZE), counts.reshape(2))))

        def hand_over(moved, pressure, moved_out, pressure_out, sem):
            first = pltpu.make_async_copy(moved, moved_out, sem.at[0])
            second = pltpu.make_async_copy(pressure, pressure_out, sem.at[1])
            first.start()
            second.start()
            first.wait()
            second.wait()

        moved, pressure = pl.pallas_call(
            hand_over,
            out_shape=(jax.ShapeDtypeStruct((3, 2, P_SIZE), F32), jax.ShapeDtypeStruct((2, P_SIZE), F32)),
            in_specs=[vmem, vmem],
            out_specs=(pl.BlockSpec(memory_space=pltpu.HBM),) * 2,
            scratch_shapes=[pltpu.SemaphoreType.DMA((2,))],
            name="hand_over",
        )(*(pltpu.with_memory_space_constraint(v, pltpu.VMEM) for v in (moved, pressure)))
        return moved.reshape(3, 1, 1, 2, P_SIZE), pressure.reshape(1, 1, 2, P_SIZE)

    return jax.shard_map(
        on_device,
        mesh=mesh,
        in_specs=(P(None, *AXES, None), P(None, *AXES, None), P(*AXES)),
        out_specs=(P(None, *AXES, None), P(*AXES, None)),
        check_vma=False,
    )
```

```python
import functools
import itertools

import jax
import jax.numpy as jnp
from jax import lax
from jax.experimental import pallas as pl
from jax.experimental.pallas import tpu as pltpu
from jax.sharding import PartitionSpec as P

P_SIZE = 128
AWAY = 64.0
DIAG_SHIFT = 0.05
VISCOSITY = 0.5
GRAVITY = 0.1
GRADIENT_GAIN = 32.0

MESH = pl.DeviceIdType.MESH
F32 = jnp.float32
AXES = ("gx", "gy", "gz")
OFFSETS = sorted((o for o in itertools.product((-1, 0, 1), repeat=3) if any(o)), key=lambda o: -sum(map(abs, o)))
N_OFF = len(OFFSETS)
OWN = 17


def pairs(own, hops):
    found = []
    for column in range(9):
        for step in range(3):
            across = abs(column // 3 - 1) + abs(column % 3 - 1) + (own + step in (0, 3))
            if across in hops:
                found.append((column * 4 + own + step, column * 3 + step))
    return found


ALL = (0, 1, 2, 3)


def kernel(sizes, pos_in, vel_in, counts_in, vel_out, pres_out, pos, vel, counts, load, x_own, x_halo, x_col, weights, sums, cols, p_own, p_halo, t_own, t_sums,
           t_halo, levered, a_own, a_halo, b_own, b_halo, send, recv, a_sem, b_sem):
    me = [lax.axis_index(axis) for axis in AXES]

    def device(offset):
        return tuple(lax.rem(m + (d + n), n) if d else m for m, d, n in zip(me, offset, sizes))

    loads = [
        pltpu.make_async_copy(a, b, load.at[i]) for i, (a, b) in enumerate(((pos_in, pos), (vel_in, vel), (counts_in, counts)))
    ]
    for item in loads:
        item.start()

    def far(offset):
        return -sum(min(d, n - d) for d, n in zip(offset, sizes))

    plane = sorted(((0, a, b) for a in range(sizes[1]) for b in range(sizes[2]) if a or b), key=far)
    length = sorted(((a, 0, 0) for a in range(1, sizes[0])), key=far)
    inside = {
        (1, -1): me[1] > 0, (1, 1): me[1] < sizes[1] - 1,
        (2, -1): me[2] > 0, (2, 1): me[2] < sizes[2] - 1,
    }

    def exists(dy, dz):
        terms = [inside[axis, d] for axis, d in ((1, dy), (2, dz)) if d]
        if not terms:
            return None
        return terms[0] if len(terms) == 1 else jnp.logical_and(*terms)

    def under(condition, body):
        if condition is None:
            body()
        else:
            pl.when(condition)(body)

    x_halo[...] = jnp.full_like(x_halo, AWAY)

    barrier = pltpu.get_barrier_semaphore()
    greeted = OFFSETS + [(3, 0, 0), (-3, 0, 0)]
    for offset in greeted:
        pl.semaphore_signal(barrier, inc=1, device_id=device(offset), device_id_type=MESH)

    p_halo[...] = jnp.zeros_like(p_halo)
    t_halo[...] = jnp.zeros_like(t_halo)
    for item in loads:
        item.wait()
    lanes = lax.broadcasted_iota(jnp.int32, (1, P_SIZE), 1)
    valid = [(lanes < counts[t]).astype(F32) for t in range(2)]
    for t in range(2):
        for k in range(3):
            x_own[t, k : k + 1] = jnp.where(valid[t] > 0, pos[k, t : t + 1], AWAY)
            x_own[t, 3 + k : 4 + k] = vel[k, t : t + 1]
        x_own[t, 6:8] = jnp.zeros((2, P_SIZE), F32)
    pl.semaphore_wait(barrier, len(greeted))

    def copy(phase, own, halo, offset):
        dx, dy, dz = offset
        place = ((1 - dx) * 3 + 1 - dy) * 4
        if dz == 0:
            source, target = own, halo.at[place + 1 : place + 3]
        elif dz > 0:
            source, target = own.at[1:2], halo.at[place : place + 1]
        else:
            source, target = own.at[0:1], halo.at[place + 3 : place + 4]
        i = OFFSETS.index(offset)
        return pltpu.make_async_remote_copy(
            source, target, send.at[phase, i], recv.at[phase, i], device_id=device(offset), device_id_type=MESH
        )

    combos = sorted(itertools.product((-1, 0, 1), repeat=2), key=lambda c: sum(map(abs, c)))

    def start(phase, own, halo):
        for dy, dz in combos:
            def body(dy=dy, dz=dz):
                for dx in (0, -1, 1):
                    if dx or dy or dz:
                        copy(phase, own, halo, (dx, dy, dz)).start()
            under(exists(dy, dz), body)

    def arrive(phase, own, halo, hops):
        for dy, dz in combos:
            steps = [dx for dx in (-1, 0, 1) if abs(dx) + abs(dy) + abs(dz) == hops]
            if steps and hops:
                def body(dy=dy, dz=dz, steps=steps):
                    for dx in steps:
                        copy(phase, own, halo, (dx, dy, dz)).wait_recv()
                under(exists(-dy, -dz), body)

    def sent(phase, own, halo):
        for dy, dz in combos:
            def body(dy=dy, dz=dz):
                for dx in (-1, 1, 0):
                    if dx or dy or dz:
                        copy(phase, own, halo, (dx, dy, dz)).wait_send()
            under(exists(dy, dz), body)

    def to_rows(n):
        for r in range(0, P_SIZE, 16):
            block = jnp.zeros((16, P_SIZE), F32)
            for a in range(2):
                for q in range(n):
                    total = jnp.sum(sums[a, q, r : r + 16], axis=1, keepdims=True)
                    block = jnp.where(lanes == 16 * a + q, total, block)
            cols[r : r + 16] = block
        turned = cols[...].T
        return [[turned[16 * a + q : 16 * a + q + 1] for q in range(n)] for a in range(2)]

    def apply(n, term, depth, exchange=None):
        for hops in ((0,), (1,), (2,), (3,)) if exchange else (ALL,):
            if exchange:
                arrive(*exchange, hops[0])

            @pl.loop(0, P_SIZE // depth)
            def _(block, hops=hops):
                at = pl.ds(pl.multiple_of(block * depth, depth), depth)
                for a in range(2):
                    if hops[0]:
                        totals = [sums[a, q, at] for q in range(n)]
                    else:
                        totals = [jnp.zeros((depth, P_SIZE), F32)] * n
                    for tile, place in pairs(a, hops):
                        terms = term(a, at, tile, place)
                        for q in range(n):
                            totals[q] = totals[q] + terms[q]
                    for q in range(n):
                        sums[a, q, at] = totals[q]
        return to_rows(n)

    def offset(a, at, tile):
        return [x_col[a, k, at] - x_halo[tile, k : k + 1] for k in range(3)]

    def weigh(a, at, tile, place):
        d = offset(a, at, tile)
        near = jnp.maximum(1.0 - (d[0] * d[0] + d[1] * d[1] + d[2] * d[2]), 0.0)
        w = near * near
        weights[a, place, at] = w
        return [w] + [w * x_halo[tile, 3 + k : 4 + k] for k in range(3)]

    def lever_terms(a, at, tile, place):
        w = weights[a, place, at]
        return [w * d for d in offset(a, at, tile)]

    def times(n, row_of):
        def term(a, at, tile, place):
            w = weights[a, place, at]
            return [w * row_of(tile, q) for q in range(n)]
        return term

    start(0, x_own, x_halo)
    for t in range(2):
        x_halo[OWN + t] = x_own[t]
        for k in range(3):
            x_col[t, k] = jnp.broadcast_to(pos[k, t : t + 1], (P_SIZE, P_SIZE)).T
    rows = apply(4, weigh, 16, (0, x_own, x_halo))
    scale = 1.0 / P_SIZE
    centre = [s * 0.5 for s in (sizes[0], sizes[1], sizes[2] * 2)]
    diagonal, predicted, x = [], [], []
    for a in range(2):
        row = rows[a][0] * valid[a]
        v = [vel[k, a : a + 1] for k in range(3)]
        x.append([pos[k, a : a + 1] - centre[k] for k in range(3)])
        diagonal.append(DIAG_SHIFT + row * scale)
        p = [valid[a] * (v[k] + VISCOSITY * scale * (rows[a][1 + k] - row * v[k]) - (GRAVITY if k == 2 else 0.0)) for k in range(3)]
        predicted.append(p)
        for k in range(3):
            p_own[a, k : k + 1] = p[k]
        p_own[a, 3:4] = p[0] * x[a][0] + p[1] * x[a][1] + p[2] * x[a][2]
    start(1, p_own, p_halo)
    p_halo[OWN : OWN + 2] = p_own[...]
    sent(0, x_own, x_halo)
    rows = apply(3, lever_terms, 16)
    lever = [[rows[a][k] * valid[a] for k in range(3)] for a in range(2)]
    rows = apply(4, times(4, lambda tile, q: p_halo[tile, q : q + 1]), 64, (1, p_own, p_halo))
    for a in range(2):
        flux = x[a][0] * rows[a][0] + x[a][1] * rows[a][1] + x[a][2] * rows[a][2] - rows[a][3]
        dot = predicted[a][0] * lever[a][0] + predicted[a][1] * lever[a][1] + predicted[a][2] * lever[a][2]
        t_own[0, a] = valid[a] * (-(GRADIENT_GAIN * scale) * (dot - flux)) / diagonal[a]
    inverse = [scale * valid[a] / diagonal[a] for a in range(2)]

    @pl.loop(0, 3)
    def _(k):
        own, halo = t_own.at[k], t_halo.at[k]
        start(2 + k, own, halo)
        halo[OWN : OWN + 2] = own[...]
        rows = apply(1, times(1, lambda tile, q: halo[tile]), 64, (2 + k, own, halo))
        for a in range(2):
            t_sums[k, a] = rows[a][0]
            t_own[k + 1, a] = rows[a][0] * inverse[a]

    basis = [[t_own[k, a] for a in range(2)] for k in range(4)]
    spread = [[t_sums[k, a] for a in range(2)] for k in range(3)]
    packed = jnp.zeros((1, P_SIZE), F32)
    for q in range(6):
        i, j = q // 2, (q + 1) // 2
        terms = sum(diagonal[a] * basis[i][a] * basis[j][a] for a in range(2))
        packed = jnp.where(lanes == q, jnp.sum(terms, axis=1, keepdims=True), packed)

    def share(peers, own, halo, sem):
        for i, offset in enumerate(peers):
            pltpu.make_async_remote_copy(
                own, halo.at[i : i + 1], sem.at[0], sem.at[1], device_id=device(offset), device_id_type=MESH
            ).start()

    def gathered(peers, own, halo, sem):
        pltpu.make_async_copy(halo, halo, sem.at[1]).wait()
        return own[0] + jnp.sum(halo[...], axis=0)

    a_own[0] = packed
    share(plane, a_own, a_halo, a_sem)

    for tile in range(36):
        local = x_halo[tile]
        for c in range(3):
            levered[c, tile] = (local[c : c + 1] - centre[c]) * jnp.concatenate([t_halo[k, tile] for k in range(3)] + [jnp.zeros((5, P_SIZE), F32)], axis=0)
    rows = apply(9, times(9, lambda tile, q: levered[q // 3, tile, q % 3 : q % 3 + 1]), 16)
    moved = []
    for a in range(2):
        moved.append([
            [basis[k][a] * lever[a][c] - valid[a] * (x[a][c] * spread[k][a] - rows[a][3 * c + k]) for k in range(3)]
            for c in range(3)
        ])

    sent(1, p_own, p_halo)
    b_own[0] = gathered(plane, a_own, a_halo, a_sem)
    share(length, b_own, b_halo, b_sem)

    @pl.loop(0, 3)
    def _(k):
        sent(2 + k, t_own.at[k], t_halo.at[k])

    pltpu.make_async_copy(a_halo, a_halo, a_sem.at[0]).wait()
    total = gathered(length, b_own, b_halo, b_sem)

    m = [jnp.sum(jnp.where(lanes == q, total, 0.0), axis=1, keepdims=True) for q in range(6)]
    g00, g01, g11, g12, g22 = (m[q] - m[q + 1] for q in range(5))
    l1, l2 = g01 / g00, g11 / g00
    a11, a12, a22 = g11 - l1 * g01, g12 - l1 * g11, g22 - l2 * g11
    y1, y2 = m[1] - l1 * m[0], m[2] - l2 * m[0]
    l3 = a12 / a11
    c2 = (y2 - l3 * y1) / (a22 - l3 * a12)
    c1 = (y1 - a12 * c2) / a11
    c0 = (m[0] - g01 * c1 - g11 * c2) / g00
    weight = [c0, c1, c2]
    for a in range(2):
        pres_out[a : a + 1] = sum(weight[k] * basis[k][a] for k in range(3))
        for c in range(3):
            vel_out[c, a : a + 1] = predicted[a][c] - (GRADIENT_GAIN * scale) * sum(weight[k] * moved[a][c][k] for k in range(3))
    pltpu.make_async_copy(b_halo, b_halo, b_sem.at[0]).wait()


def solution(mesh):
    sizes = tuple(mesh.shape[axis] for axis in AXES)

    def on_device(positions, velocity, counts):
        vmem = pl.BlockSpec(memory_space=pltpu.VMEM)
        n_plane, n_length = sizes[1] * sizes[2] - 1, sizes[0] - 1
        moved, pressure = pl.pallas_call(
            functools.partial(kernel, sizes),
            out_shape=(jax.ShapeDtypeStruct((3, 2, P_SIZE), F32), jax.ShapeDtypeStruct((2, P_SIZE), F32)),
            in_specs=[pl.BlockSpec(memory_space=pltpu.HBM)] * 3,
            out_specs=(vmem, vmem),
            scratch_shapes=[
                pltpu.VMEM((3, 2, P_SIZE), F32),
                pltpu.VMEM((3, 2, P_SIZE), F32),
                pltpu.SMEM((2,), jnp.int32),
                pltpu.SemaphoreType.DMA((3,)),
                pltpu.VMEM((2, 8, P_SIZE), F32),
                pltpu.VMEM((36, 8, P_SIZE), F32),
                pltpu.VMEM((2, 3, P_SIZE, P_SIZE), F32),
                pltpu.VMEM((2, 27, P_SIZE, P_SIZE), F32),
                pltpu.VMEM((2, 9, P_SIZE, P_SIZE), F32),
                pltpu.VMEM((P_SIZE, P_SIZE), F32),
                pltpu.VMEM((2, 4, P_SIZE), F32),
                pltpu.VMEM((36, 4, P_SIZE), F32),
                pltpu.VMEM((4, 2, 1, P_SIZE), F32),
                pltpu.VMEM((3, 2, 1, P_SIZE), F32),
                pltpu.VMEM((3, 36, 1, P_SIZE), F32),
                pltpu.VMEM((3, 36, 8, P_SIZE), F32),
                pltpu.VMEM((1, 1, P_SIZE), F32),
                pltpu.VMEM((n_plane, 1, P_SIZE), F32),
                pltpu.VMEM((1, 1, P_SIZE), F32),
                pltpu.VMEM((n_length, 1, P_SIZE), F32),
                pltpu.SemaphoreType.DMA((5, N_OFF)),
                pltpu.SemaphoreType.DMA((5, N_OFF)),
                pltpu.SemaphoreType.DMA((2,)),
                pltpu.SemaphoreType.DMA((2,)),
            ],
            compiler_params=pltpu.CompilerParams(
                collective_id=0, has_side_effects=True, vmem_limit_bytes=32 * 1024 * 1024
            ),
            name="project",
        )(*(pltpu.with_memory_space_constraint(v, pltpu.HBM) for v in (positions.reshape(3, 2, P_SIZE), velocity.reshape(3, 2, P_SIZE), counts.reshape(2))))
        return moved.reshape(3, 1, 1, 2, P_SIZE), pressure.reshape(1, 1, 2, P_SIZE)

    return jax.shard_map(
        on_device,
        mesh=mesh,
        in_specs=(P(None, *AXES, None), P(None, *AXES, None), P(*AXES)),
        out_specs=(P(None, *AXES, None), P(*AXES, None)),
        check_vma=False,
    )
```
